128 devices in a mesh: grp: 4 (over y_hi, core), fsdp: 32 (over x, y_lo, z).
Axes of the slice: x: 4, y: 4 (y_hi: 2, y_lo: 2; y = y_hi * 2 + y_lo), z: 4, core: 2. Of those that a mesh axis runs over, the one named last changes fastest.
Arguments:
- small_w: bfloat16 [4, 4096, 4096], P('grp', 'fsdp'), may hold values from -0.09375 to 0.09375
- small_m: float32 [4, 4096, 4096], P('grp', 'fsdp'), may hold values from -6 to 6
- small_v: float32 [4, 4096, 4096], P('grp', 'fsdp'), may hold values from 0 to 1, as said below
- width_map: bfloat16 [2560, 4096], P(('grp', 'fsdp')), may hold values from -1 to 1
- head_map: float32 [40, 32], replicated, may hold values from -1 to 1
- layer_slot: int32 [4], replicated, may hold values from 0 to 3, each once
- depth_src: int32 [5, 2], replicated, may hold values from 0 to 3, as said below
- depth_coef: float32 [5, 2], replicated, may hold values from 0.3 to 1
Outputs:
- grown_w: bfloat16 [5, 5120, 2560], P(None, ('grp', 'fsdp'))
- grown_m: float32 [5, 5120, 2560], P(None, ('grp', 'fsdp'))
- grown_v: float32 [5, 5120, 2560], P(None, ('grp', 'fsdp'))
The draws below stay inside these ranges and needn't reach their ends.
Inputs may be any that keep to these rules, and one draw needn't show every extreme that they name: `layer_slot`: each source layer fills exactly one slot. `depth_src`: the first source of grown layer j is j * 4 // 5. `small_v`: positive.
All inputs are finite; a program needn't handle non-finite values.
Results may differ from the reference program's by a relative error of at most 0.0057.
Values may be sent and summed in bfloat16 or wider, within the bound.
No kernel may reach another device: no remote copies, remote signals or barrier semaphores. Data moves between devices by JAX's collectives and lax.ppermute only.
A program may use at most 256 MiB of HBM per device.

```python
import jax
import jax.numpy as jnp
from jax import lax

HEADS_S = 32
HEADS_G = 40
COLS_S = 4096
COLS_G = 2560
LS = 4
LG = 5
R_S = 4096


def draw_depth_src(key, part):
    key = jax.random.fold_in(key, 7)
    first = jnp.arange(LG) * LS // LG
    second = jax.random.randint(key, (LG,), 0, LS)
    return jnp.stack([first, second], axis=1).astype(jnp.int32)


def draw_width_map(key, part):
    key = jax.random.fold_in(key, 11)
    key_level, key_base = jax.random.split(key)
    levels = jax.random.uniform(key_level, (32, 32), jnp.float32, -1.5, 1.5)
    row_block = jnp.arange(COLS_G) * 32 // COLS_G
    col_block = jnp.arange(COLS_S) * 32 // COLS_S
    factor = jnp.exp(levels[row_block][:, col_block])
    base = jax.random.truncated_normal(key_base, -3.0, 3.0, (COLS_G, COLS_S), jnp.float32)
    values = jnp.clip(base * factor * float(COLS_S) ** (-0.5), -1.0, 1.0)
    return values.astype(jnp.bfloat16)


def draw_small_v(key, part):
    key = jax.random.fold_in(key, 13)
    key_level, key_base = jax.random.split(key)
    col_block = jnp.arange(COLS_S) * 32 // COLS_S
    levels = jax.random.uniform(key_level, (LS, 32), jnp.float32, -2.3, 0.0)
    base = jax.random.uniform(key_base, (LS, R_S, COLS_S), jnp.float32, -2.3, 0.0)
    return jnp.exp(base + levels[:, None, :][:, :, col_block]).astype(jnp.float32)


def block_levels(key, shape, pieces, low, largest):
    def one(position, blocks):
        steps = jax.random.uniform(jax.random.fold_in(jax.random.fold_in(key, 6), position), (blocks,), jnp.float32, low / len(pieces), largest / len(pieces))
        return jnp.repeat(jnp.exp(steps), shape[position] // blocks).reshape((-1,) + (1,) * (len(shape) - position - 1))

    factor_of = one(*pieces[0])
    for cut in pieces[1:]:
        factor_of = factor_of * one(*cut)
    return factor_of


def bell_draw(key, shape, deviation, bound, cuts=(), dtype=jnp.bfloat16):
    loudness = block_levels(key, shape, cuts, -0.22, 0.18) if cuts else 1.0
    array = jax.random.normal(key, shape, jnp.float32) * deviation * loudness
    return jnp.minimum(jnp.maximum(array, -bound), bound).astype(dtype)


def setup_inputs(seed: int = 0) -> dict:
    key_of = jax.random.split(jax.random.key(seed), 9)
    return {
        "small_w": bell_draw(key_of[0], (LS, R_S, COLS_S), COLS_S ** -0.5, 0.09375, ((0, 4), (1, 32))),
        "small_m": bell_draw(key_of[1], (LS, R_S, COLS_S), 1.0, 6.0, ((0, 4), (1, 32)), jnp.float32),
        "small_v": draw_small_v(jax.random.fold_in(key_of[8], 71), 0),
        "width_map": draw_width_map(jax.random.fold_in(key_of[8], 71), 0),
        "head_map": bell_draw(key_of[4], (HEADS_G, HEADS_S), HEADS_S ** -0.5, 1.0, (), jnp.float32),
        "layer_slot": jax.random.permutation(key_of[5], LS).astype(jnp.int32),
        "depth_src": draw_depth_src(jax.random.fold_in(key_of[8], 71), 0),
        "depth_coef": jnp.clip(jax.random.uniform(key_of[7], (LG, 2), jnp.float32, 0.3, 1.0), 0.3, 1.0),
    }


def depth_matrix(layer_slot, depth_src, depth_coef):
    hits = (layer_slot[None, None, :] == depth_src[:, :, None]).astype(jnp.float32)
    return jnp.sum(depth_coef[:, :, None] * hits, axis=1)


def project(left, right, exact):
    dims = (((left.ndim - 1,), (1,)), ((), ()))
    if exact:
        return lax.dot_general(left, right, dims, precision=lax.Precision.HIGHEST, preferred_element_type=jnp.float32)
    return lax.dot_general(left, right, dims, preferred_element_type=jnp.float32)


def mix_heads(block, matrix):
    shape = block.shape
    heads = matrix.shape[1]
    split = block.reshape(shape[:-2] + (heads, shape[-2] // heads, shape[-1]))
    mixed = jnp.einsum('gh,...hdc->...gdc', matrix, split, precision=lax.Precision.HIGHEST)
    return mixed.reshape(shape[:-2] + (matrix.shape[0] * (shape[-2] // heads), shape[-1]))


def reference(small_w, small_m, small_v, width_map, head_map, layer_slot, depth_src, depth_coef):
    depth = depth_matrix(layer_slot, depth_src, depth_coef)
    wide = width_map.astype(jnp.float32)
    wide_sq = wide * wide
    head_sq = head_map * head_map
    list_w, list_m, list_v = [], [], []
    for slot in range(LS):
        z_w = project(small_w[slot], width_map, False).astype(jnp.bfloat16)
        z_w = lax.optimization_barrier(z_w).astype(jnp.float32)
        z_m = project(small_m[slot], wide, True)
        z_v = project(small_v[slot], wide_sq, True)
        y_w = mix_heads(z_w, head_map).astype(jnp.bfloat16)
        list_w.append(lax.optimization_barrier(y_w).astype(jnp.float32))
        list_m.append(mix_heads(z_m, head_map))
        list_v.append(mix_heads(z_v, head_sq))
    stack_w = jnp.stack(list_w)
    stack_m = jnp.stack(list_m)
    stack_v = jnp.stack(list_v)
    hi = lax.Precision.HIGHEST
    grown_w = jnp.einsum('js,src->jrc', depth, stack_w, precision=hi).astype(jnp.bfloat16)
    grown_m = jnp.einsum('js,src->jrc', depth, stack_m, precision=hi)
    grown_v = jnp.einsum('js,src->jrc', depth * depth, stack_v, precision=hi)
    return grown_w, grown_m, grown_v
```

```python
import jax
import jax.numpy as jnp
from jax import lax
from jax.experimental import pallas as pl
from jax.experimental.pallas import tpu as pltpu
from jax.sharding import Mesh, PartitionSpec as P

SIZES = (2, 2, 4, 2, 4)
AXES = ("yh", "core", "x", "yl", "z")
GROUP = ("x", "yl", "z")
BF16, F32 = jnp.bfloat16, jnp.float32

COLS, HALF, DEPTH = 2560, 1280, 4096
BLOCK = 80
UNITS = 64
VMEM = 56 * 1024 * 1024


def place(yh, core, x, yl, z):
    return (((yh * 2 + core) * 4 + x) * 2 + yl) * 4 + z


def shift(value, axis_of_core, by):
    pairs = []
    for yh in range(2):
        for core in range(2):
            for x in range(4):
                for yl in range(2):
                    for z in range(4):
                        to = [x, 2 * yh + yl]
                        to[axis_of_core[core]] = (to[axis_of_core[core]] + by) % 4
                        pairs.append(
                            (place(yh, core, x, yl, z), place(to[1] // 2, core, to[0], to[1] % 2, z))
                        )
    return lax.ppermute(value, AXES, pairs)


def gather_width(shard):
    block = lax.all_gather(shard, "z", axis=0, tiled=True)
    first, second = (1, 0), (0, 1)
    before, after, across = (
        shift(block, first, 1),
        shift(block, first, -1),
        shift(block, first, 2),
    )
    a = jnp.concatenate([block, before], axis=0)
    b = jnp.concatenate([after, across], axis=0)
    ra, lb = shift(a, second, 1), shift(b, second, -1)
    rb, la = shift(b, second, 1), shift(a, second, -1)
    pieces = [a, b, ra, rb, la, lb, shift(ra, second, 1), shift(lb, second, -1)]
    core = lax.axis_index("core")
    x = lax.axis_index("x")
    y = lax.axis_index("yh") * 2 + lax.axis_index("yl")
    rows = []
    for late in (0, -1, 1, 2):
        for early in (0, -1, 1, 2):
            bx = (x + jnp.where(core == 0, late, early)) % 4
            by = (y + jnp.where(core == 0, early, late)) % 4
            rows.append(((by // 2) * 8 + bx * 2 + by % 2) * BLOCK)
    return pieces, jnp.stack(rows).astype(jnp.int32)


def widen_kernel(rows, own, other, *refs):
    pieces, out = refs[:8], refs[8]
    b_ref, a_ref, b_sem, a_sem = refs[9:]
    copies = []
    for i, (src, dst) in enumerate(
        (
            (own.at[0:2], a_ref.at[0:2]),
            (other.at[0:2], a_ref.at[2:4]),
            (own.at[2:3], a_ref.at[4:5]),
            (other.at[2:3], a_ref.at[5:6]),
        )
    ):
        copies.append(pltpu.make_async_copy(src, dst, a_sem.at[i]))
    for i in range(16):
        copies.append(
            pltpu.make_async_copy(
                pieces[i // 2].at[pl.ds((i % 2) * BLOCK, BLOCK)],
                b_ref.at[pl.ds(pl.multiple_of(rows[i], 16), BLOCK)],
                b_sem.at[i],
            )
        )
    for copy in copies:
        copy.start()
    for copy in copies:
        copy.wait()
    nt = (((1,), (1,)), ((), ()))

    @pl.loop(0, HALF // 256)
    def _(tile):
        b = b_ref[pl.ds(pl.multiple_of(tile * 256, 256), 256), :]
        wm = lax.dot_general(
            a_ref[0:4].reshape(512, DEPTH), b, nt, preferred_element_type=F32
        ).astype(BF16)
        v = lax.dot_general(
            a_ref[4:6].reshape(256, DEPTH), b * b, nt, preferred_element_type=F32
        ).astype(BF16)
        for half in range(2):
            cols = slice(half * 128, half * 128 + 128)
            t = tile * 2 + half
            out[t] = wm[0:128, cols]
            out[10 + t] = wm[128:256, cols]
            out[20 + t] = v[0:128, cols]
            out[30 + t] = wm[256:384, cols]
            out[40 + t] = wm[384:512, cols]
            out[50 + t] = v[128:256, cols]

    out[60:64] = jnp.zeros((4, 128, 128), BF16)


def widen(rows, own, other, pieces):
    anywhere = pl.BlockSpec(memory_space=pl.ANY)
    return pl.pallas_call(
        widen_kernel,
        out_shape=jax.ShapeDtypeStruct((UNITS, 128, 128), BF16),
        in_specs=[pl.BlockSpec(memory_space=pltpu.SMEM)] + [anywhere] * 10,
        out_specs=pl.BlockSpec(memory_space=pltpu.VMEM),
        scratch_shapes=[
            pltpu.VMEM((HALF, DEPTH), BF16),
            pltpu.VMEM((6, 128, DEPTH), BF16),
            pltpu.SemaphoreType.DMA((16,)),
            pltpu.SemaphoreType.DMA((4,)),
        ],
        compiler_params=pltpu.CompilerParams(vmem_limit_bytes=VMEM),
        cost_estimate=pl.CostEstimate(
            flops=2 * 768 * HALF * DEPTH, bytes_accessed=20 << 20, transcendentals=0
        ),
        name="widen",
    )(rows, own, other, *pieces)


def mix_kernel(z_ref, m_ref, out, y_ref):
    for k in range(2):

        @pl.loop(0, 4)
        def _(pair):
            row = pl.multiple_of(pair * 32, 32)
            block = jnp.concatenate(
                [z_ref[:, k, pl.ds(row + 16 * i, 16), :].reshape(512, 128) for i in range(2)], axis=1
            )
            y = jnp.dot(m_ref[0], block, preferred_element_type=F32)
            y = y + jnp.dot(m_ref[1], block, preferred_element_type=F32)
            for g in range(40):
                for i in range(2):
                    y_ref[k, pl.ds(g * 128 + row + 16 * i, 16), :] = y[
                        g * 16 : g * 16 + 16, i * 128 : i * 128 + 128
                    ]

    @pl.loop(0, 128, unroll=4)
    def _(d):
        row = pl.multiple_of(d * 40, 8)
        both = jnp.concatenate([y_ref[k, pl.ds(row, 40), :] for k in range(2)], axis=0)
        out[d] = both.astype(BF16)


def mix(z, matrices):
    whole = pl.BlockSpec(memory_space=pltpu.VMEM)
    return pl.pallas_call(
        mix_kernel,
        out_shape=jax.ShapeDtypeStruct((128, 80, 128), BF16),
        in_specs=[whole] * 2,
        out_specs=whole,
        scratch_shapes=[pltpu.VMEM((2, 5120, 128), F32)],
        compiler_params=pltpu.CompilerParams(vmem_limit_bytes=VMEM),
        cost_estimate=pl.CostEstimate(
            flops=16 * 4 * 640 * 512 * 128, bytes_accessed=8 << 20, transcendentals=0
        ),
        name="mix",
    )(z, matrices)


def matrix_kernel(squared, head, out):
    h = head[...]
    h = jnp.where(squared[0] == 1, h * h, h)
    high = h.astype(BF16)
    low = (h - high.astype(F32)).astype(BF16)

    def iota(shape, dim):
        return lax.broadcasted_iota(jnp.int32, shape, dim)

    down = (iota((640, 40), 0) // 16 == iota((640, 40), 1)).astype(BF16)
    along = (iota((32, 512), 1) // 16 == iota((32, 512), 0)).astype(BF16)
    same = iota((640, 512), 0) % 16 == iota((640, 512), 1) % 16
    for i, part in enumerate((high, low)):
        tall = jnp.dot(down, part, preferred_element_type=F32).astype(BF16)
        full = jnp.dot(tall, along, preferred_element_type=F32)
        out[i] = jnp.where(same, full, 0.0).astype(BF16)


def mixing_matrices(head_map):
    f = (lax.axis_index("x") * 2 + lax.axis_index("yl")) * 4 + lax.axis_index("z")
    squared = ((2 * f % 30) // 10 == 2).astype(jnp.int32).reshape(1)
    whole = pl.BlockSpec(memory_space=pltpu.VMEM)
    return pl.pallas_call(
        matrix_kernel,
        out_shape=jax.ShapeDtypeStruct((2, 640, 512), BF16),
        in_specs=[pl.BlockSpec(memory_space=pltpu.SMEM), whole],
        out_specs=whole,
        compiler_params=pltpu.CompilerParams(vmem_limit_bytes=VMEM),
        name="matrices",
    )(squared, head_map)


def depth_kernel(depth, r_ref, out_w, out_m, out_v):
    @pl.loop(0, 10)
    def _(step):
        core, pair = step // 5, step % 5
        starts = []
        for k in range(2):
            t = 2 * pair + k
            starts.append(pl.multiple_of(((t // 5) * 10 + core * 5 + t % 5) * 128, 128))
        for tensor, out in enumerate((out_w, out_m, out_v)):
            terms = []
            for yh in range(2):
                for rel in range(2):
                    src = (yh * 2 + core) * 32 + rel * 15 + tensor * 5 + pair
                    slot = 2 * yh + (rel + core) % 2
                    terms.append((slot, r_ref[src].astype(F32)))
            for j in range(5):
                total = None
                for slot, value in terms:
                    c = depth[j, slot]
                    c = c * c if tensor == 2 else c
                    total = c * value if total is None else total + c * value
                for k in range(2):
                    out[j, :, pl.ds(starts[k], 128)] = total[k * 40 : k * 40 + 40].astype(out.dtype)


def mix_depth(depth, received):
    whole = pl.BlockSpec(memory_space=pltpu.VMEM)
    return pl.pallas_call(
        depth_kernel,
        out_shape=tuple(jax.ShapeDtypeStruct((5, 40, COLS), dt) for dt in (BF16, F32, F32)),
        in_specs=[pl.BlockSpec(memory_space=pltpu.SMEM), whole],
        out_specs=(whole,) * 3,
        compiler_params=pltpu.CompilerParams(vmem_limit_bytes=VMEM),
        cost_estimate=pl.CostEstimate(flops=12 << 20, bytes_accessed=8 << 20, transcendentals=0),
        name="depth",
    )(depth, received)


def depth_matrix(layer_slot, depth_src, depth_coef):
    hits = (layer_slot[None, None, :] == depth_src[:, :, None]).astype(F32)
    return jnp.sum(depth_coef[:, :, None] * hits, axis=1)


def on_device(small_w, small_m, small_v, width_map, head_map, layer_slot, depth_src, depth_coef):
    own = jnp.concatenate([small_w, small_m.astype(BF16), small_v.astype(BF16)], axis=0)
    other = lax.ppermute(own, "core", ((0, 1), (1, 0)))
    pieces, rows = gather_width(width_map)
    z = widen(rows, own, other, pieces).reshape(32, 2, 128, 128)
    z = lax.all_to_all(z, GROUP, split_axis=0, concat_axis=0, tiled=True)
    y = mix(z, mixing_matrices(head_map))
    received = lax.all_to_all(y, AXES, split_axis=0, concat_axis=0, tiled=True)
    return mix_depth(depth_matrix(layer_slot, depth_src, depth_coef), received)


def solution(mesh):
    chips = Mesh(mesh.devices.reshape(SIZES), AXES)
    grp, fsdp = ("yh", "core"), GROUP
    return jax.shard_map(
        on_device,
        mesh=chips,
        in_specs=(
            P(grp, fsdp, None),
            P(grp, fsdp, None),
            P(grp, fsdp, None),
            P(AXES, None),
            P(),
            P(),
            P(),
            P(),
        ),
        out_specs=(P(None, AXES, None),) * 3,
        check_vma=False,
    )
```

```python
import jax
import jax.numpy as jnp
from jax import lax
from jax.experimental import pallas as pl
from jax.experimental.pallas import tpu as pltpu
from jax.sharding import Mesh, PartitionSpec as P

SIZES = (2, 2, 4, 2, 4)
AXES = ("yh", "core", "x", "yl", "z")
GROUP = ("x", "yl", "z")
BF16, F32 = jnp.bfloat16, jnp.float32

COLS, HALF, DEPTH = 2560, 1280, 4096
BLOCK = 80
UNITS = 64
VMEM = 26 * 1024 * 1024


def place(yh, core, x, yl, z):
    return (((yh * 2 + core) * 4 + x) * 2 + yl) * 4 + z


def shift(value, axis_of_core, by):
    pairs = []
    for yh in range(2):
        for core in range(2):
            for x in range(4):
                for yl in range(2):
                    for z in range(4):
                        to = [x, 2 * yh + yl]
                        to[axis_of_core[core]] = (to[axis_of_core[core]] + by) % 4
                        pairs.append(
                            (place(yh, core, x, yl, z), place(to[1] // 2, core, to[0], to[1] % 2, z))
                        )
    return lax.ppermute(value, AXES, pairs)


def order_kernel(mine, own, before, after, across, out, wide, block, sem):
    for at in range(4):
        for by, shard in ((0, own), (1, after), (2, across), (3, before)):

            @pl.when((at - mine[0] + 4) % 4 == by)
            def _():
                wide[20 * at : 20 * at + 20, :] = shard[...].astype(F32)

    block[...] = wide[...].astype(BF16)
    copy = pltpu.make_async_copy(block, out, sem)
    copy.start()
    copy.wait()


def in_order(mine, *shards):
    whole = pl.BlockSpec(memory_space=pltpu.VMEM)
    return pl.pallas_call(
        order_kernel,
        out_shape=jax.ShapeDtypeStruct((BLOCK, DEPTH), BF16),
        in_specs=[pl.BlockSpec(memory_space=pltpu.SMEM)] + [whole] * 4,
        out_specs=pl.BlockSpec(memory_space=pltpu.HBM),
        scratch_shapes=[
            pltpu.VMEM((BLOCK, DEPTH), F32),
            pltpu.VMEM((BLOCK, DEPTH), BF16),
            pltpu.SemaphoreType.DMA,
        ],
        compiler_params=pltpu.CompilerParams(vmem_limit_bytes=VMEM),
        name="order",
    )(mine, *shards)


def once(value, *done):
    return lax.optimization_barrier((value, *done))[0]


def grow_width(shard, small_w, small_m, small_v):
    core, z = lax.axis_index("core"), lax.axis_index("z")
    x = lax.axis_index("x")
    y = lax.axis_index("yh") * 2 + lax.axis_index("yl")
    q, p = jnp.where(core == 0, x, y), jnp.where(core == 0, y, x)

    def along_p(value, by):
        return shift(value, (1, 0), by)

    def along_q(value, by):
        return shift(value, (0, 1), by)

    def along_z(value, by):
        return lax.ppermute(value, "z", [(i, (i + by) % 4) for i in range(4)])

    before, after, across = along_p(shard, 1), along_p(shard, -1), along_p(shard, 2)
    own = jnp.concatenate([small_w, small_m.astype(BF16), small_v.astype(BF16)], axis=0)
    other = lax.ppermute(own, "core", ((0, 1), (1, 0)))
    a = in_order(p.reshape(1), shard, before, after, across)
    a_before, a_after = along_q(a, 1), along_q(a, -1)
    b_before, b_after = along_z(a, 1), along_z(a, -1)
    a_across = along_q(a_before, 1)
    b = once(jnp.concatenate([b_before, b_after], axis=0), a_across, a_after, other)
    d = along_z(once(a, b_before), 2)
    b_before, b_after = along_q(b, 1), along_q(b, -1)
    here = jnp.stack([core, q, z]).astype(jnp.int32)
    first = (
        (a, b, a_before, a_after, a_across),
        ((0, 0), (0, -1), (0, 1), (-1, 0), (1, 0), (2, 0)),
    )
    z_first = widen(own, other, first)
    d_sent = once(d, z_first)
    d_before, d_after = along_q(d_sent, 1), along_q(d_sent, -1)
    second = ((d, b_before, b_after), ((0, 2), (-1, -1), (-1, 1), (1, -1), (1, 1)))
    b_across = along_q(b_after, -1)
    z_second = widen(own, other, second)
    d_across = along_q(once(d_before, z_second), 1)
    last = (
        (b_across, d_before, d_after, d_across),
        ((2, -1), (2, 1), (-1, 2), (1, 2), (2, 2)),
    )
    partial = spread((first[1], second[1]), (z_first, z_second), here)
    return widen_last(own, other, last, partial, here)


def load_and_project(own, other, pieces, b_ref, a_ref, b_sem, a_sem):
    copies = []
    row = 0
    for i, piece in enumerate(pieces):
        rows = piece.shape[0]
        copies.append(pltpu.make_async_copy(piece, b_ref.at[pl.ds(row, rows)], b_sem.at[i]))
        row += rows
    for i, (src, dst) in enumerate(
        (
            (own.at[0:2], a_ref.at[0:2]),
            (other.at[0:2], a_ref.at[2:4]),
            (own.at[2:3], a_ref.at[4:5]),
            (other.at[2:3], a_ref.at[5:6]),
        )
    ):
        copies.append(pltpu.make_async_copy(src, dst, a_sem.at[i]))
    for copy in copies:
        copy.start()
    for copy in copies:
        copy.wait()
    nt = (((1,), (1,)), ((), ()))
    b = b_ref[...]
    wm = lax.dot_general(a_ref[0:4].reshape(512, DEPTH), b, nt, preferred_element_type=F32)
    v = lax.dot_general(a_ref[4:6].reshape(256, DEPTH), b * b, nt, preferred_element_type=F32)
    return wm.astype(BF16), v.astype(BF16)


def widen_kernel(n, own, other, *refs):
    wm, v = load_and_project(own, other, refs[:n], *refs[n + 1 :])
    refs[n][0:512] = wm
    refs[n][512:768] = v


def spread_columns(places, values, here, previous, out):
    core, q, z = here[0], here[1], here[2]
    row = lax.broadcasted_iota(jnp.int32, (BLOCK, 256), 0)
    lane = lax.broadcasted_iota(jnp.int32, (BLOCK, 256), 1)
    third = [(row >= 20 * k).astype(jnp.int32) for k in (1, 2, 3)]
    line = third[0] + third[1] + third[2]
    inner = row - 20 * line
    spot = (
        inner
        + jnp.where(core == 0, third[1] * 640 + (line - 2 * third[1]) * 80, line * 160)
        - lane
    )

    @pl.loop(0, HALF // 256)
    def _(tile):
        total = None
        for group, value in zip(places, values):
            ones = []
            for dq, dz in group:
                bq, bz = lax.rem(q + dq + 4, 4), lax.rem(z + dz + 4, 4)
                base = bz * 20 + jnp.where(
                    core == 0, bq * 160, (bq // 2) * 640 + lax.rem(bq, 2) * 80
                )
                ones.append(jnp.where(spot == tile * 256 - base, 1.0, 0.0).astype(BF16))
            moved = jnp.dot(
                value[...], jnp.concatenate(ones, axis=0), preferred_element_type=F32
            )
            total = moved if total is None else total + moved
        total = total.astype(BF16)
        for first, at in ((0, 0), (10, 1), (20, 4), (30, 2), (40, 3), (50, 5)):
            for half in range(2):
                t = first + tile * 2 + half
                part = total[at * 128 : at * 128 + 128, half * 128 : half * 128 + 128]
                out[t] = part if previous is None else previous[t] + part

    out[60:64] = jnp.zeros((4, 128, 128), BF16)


def spread(places, values, here):
    def kernel(here, *refs):
        spread_columns(places, refs[:-1], here, None, refs[-1])

    whole = pl.BlockSpec(memory_space=pltpu.VMEM)
    rows = BLOCK * sum(len(group) for group in places)
    return pl.pallas_call(
        kernel,
        out_shape=jax.ShapeDtypeStruct((UNITS, 128, 128), BF16),
        in_specs=[pl.BlockSpec(memory_space=pltpu.SMEM)] + [whole] * len(values),
        out_specs=whole,
        compiler_params=pltpu.CompilerParams(vmem_limit_bytes=VMEM),
        cost_estimate=pl.CostEstimate(
            flops=2 * 768 * rows * HALF, bytes_accessed=4 << 20, transcendentals=0
        ),
        name="spread",
    )(here, *values)


def last_kernel(n, places, here, own, other, *refs):
    last = refs[-1]
    wm, v = load_and_project(own, other, refs[:n], *refs[n + 2 : -1])
    last[0:512] = wm
    last[512:768] = v
    spread_columns([places], [last], here, refs[n], refs[n + 1])


def project_call(kernel, operands, specs, out, rows, n, more_scratch, flops, name):
    return pl.pallas_call(
        kernel,
        out_shape=jax.ShapeDtypeStruct(out, BF16),
        in_specs=specs,
        out_specs=pl.BlockSpec(memory_space=pltpu.VMEM),
        scratch_shapes=[
            pltpu.VMEM((rows, DEPTH), BF16),
            pltpu.VMEM((6, 128, DEPTH), BF16),
            pltpu.SemaphoreType.DMA((n,)),
            pltpu.SemaphoreType.DMA((4,)),
            *more_scratch,
        ],
        compiler_params=pltpu.CompilerParams(vmem_limit_bytes=VMEM),
        cost_estimate=pl.CostEstimate(
            flops=2 * 768 * rows * DEPTH + flops, bytes_accessed=10 << 20, transcendentals=0
        ),
        name=name,
    )(*operands)


def widen(own, other, group):
    pieces, places = group
    n, rows = len(pieces), len(places) * BLOCK

    def kernel(*refs):
        widen_kernel(n, *refs)

    return project_call(
        kernel,
        (own, other, *pieces),
        [pl.BlockSpec(memory_space=pl.ANY)] * (2 + n),
        (768, rows),
        rows,
        n,
        (),
        0,
        "widen",
    )


def widen_last(own, other, group, partial, here):
    pieces, places = group
    n, rows = len(pieces), len(places) * BLOCK

    def kernel(*refs):
        last_kernel(n, places, *refs)

    whole = pl.BlockSpec(memory_space=pltpu.VMEM)
    return project_call(
        kernel,
        (here, own, other, *pieces, partial),
        [pl.BlockSpec(memory_space=pltpu.SMEM)] + [pl.BlockSpec(memory_space=pl.ANY)] * (2 + n) + [whole],
        (UNITS, 128, 128),
        rows,
        n,
        (pltpu.VMEM((768, rows), BF16),),
        2 * 768 * HALF * rows,
        "widen_last",
    )


def mix_kernel(z_ref, m_ref, out, y_ref):
    row = pl.multiple_of(pl.program_id(0) * 32, 32)
    for k in range(2):
        block = jnp.concatenate(
            [z_ref[:, k, pl.ds(row + 16 * i, 16), :].reshape(512, 128) for i in range(2)], axis=1
        )
        y = jnp.dot(m_ref[0], block, preferred_element_type=F32)
        y = y + jnp.dot(m_ref[1], block, preferred_element_type=F32)
        for g in range(40):
            for i in range(2):
                y_ref[k, pl.ds(g * 128 + row + 16 * i, 16), :] = y[
                    g * 16 : g * 16 + 16, i * 128 : i * 128 + 128
                ]

    @pl.when(pl.program_id(0) == 3)
    def _():
        @pl.loop(0, 128, unroll=8)
        def _(d):
            first = pl.multiple_of(d * 40, 8)
            both = jnp.concatenate([y_ref[k, pl.ds(first, 40), :] for k in range(2)], axis=0)
            out[d] = both.astype(BF16)


def mix(z, matrices):
    return pl.pallas_call(
        mix_kernel,
        out_shape=jax.ShapeDtypeStruct((128, 80, 128), BF16),
        grid=(4,),
        in_specs=[
            pl.BlockSpec(memory_space=pltpu.VMEM),
            pl.BlockSpec(memory_space=pltpu.VMEM),
        ],
        out_specs=pl.BlockSpec(memory_space=pltpu.VMEM),
        scratch_shapes=[pltpu.VMEM((2, 5120, 128), F32)],
        compiler_params=pltpu.CompilerParams(vmem_limit_bytes=VMEM),
        cost_estimate=pl.CostEstimate(
            flops=16 * 4 * 640 * 512 * 128, bytes_accessed=8 << 20, transcendentals=0
        ),
        name="mix",
    )(z, matrices)


def matrix_kernel(squared, head, out):
    h = head[...]
    h = jnp.where(squared[0] == 1, h * h, h)
    high = h.astype(BF16)
    low = (h - high.astype(F32)).astype(BF16)

    def iota(shape, dim):
        return lax.broadcasted_iota(jnp.int32, shape, dim)

    down = (iota((640, 40), 0) // 16 == iota((640, 40), 1)).astype(BF16)
    along = (iota((32, 512), 1) // 16 == iota((32, 512), 0)).astype(BF16)
    same = iota((640, 512), 0) % 16 == iota((640, 512), 1) % 16
    for i, part in enumerate((high, low)):
        tall = jnp.dot(down, part, preferred_element_type=F32).astype(BF16)
        full = jnp.dot(tall, along, preferred_element_type=F32)
        out[i] = jnp.where(same, full, 0.0).astype(BF16)


def mixing_matrices(head_map):
    f = (lax.axis_index("x") * 2 + lax.axis_index("yl")) * 4 + lax.axis_index("z")
    squared = ((2 * f % 30) // 10 == 2).astype(jnp.int32).reshape(1)
    whole = pl.BlockSpec(memory_space=pltpu.VMEM)
    return pl.pallas_call(
        matrix_kernel,
        out_shape=jax.ShapeDtypeStruct((2, 640, 512), BF16),
        in_specs=[pl.BlockSpec(memory_space=pltpu.SMEM), whole],
        out_specs=whole,
        compiler_params=pltpu.CompilerParams(vmem_limit_bytes=VMEM),
        name="matrices",
    )(squared, head_map)


def depth_kernel(depth, r_ref, out_w, out_m, out_v):
    core = pl.program_id(0)
    for y_half in range(2):

        @pl.when(pl.program_id(1) == y_half)
        def _():
            for i in range(5):
                pair, k = divmod(y_half * 5 + i, 2)
                for tensor, out in enumerate((out_w, out_m, out_v)):
                    values = [
                        r_ref[yh, core, rel * 15 + tensor * 5 + pair].astype(F32)[k * 40 : k * 40 + 40]
                        for yh in range(2)
                        for rel in range(2)
                    ]
                    for j in range(5):
                        total = None
                        for n, value in enumerate(values):
                            yh, rel = divmod(n, 2)
                            c = depth[j, 2 * yh + lax.rem(rel + core, 2)]
                            c = c * c if tensor == 2 else c
                            total = c * value if total is None else total + c * value
                        out[j, :, i * 128 : i * 128 + 128] = total.astype(out.dtype)


def mix_depth(depth, received):
    block = pl.BlockSpec((5, 40, 640), lambda core, y_half: (0, 0, 2 * y_half + core))
    return pl.pallas_call(
        depth_kernel,
        out_shape=tuple(jax.ShapeDtypeStruct((5, 40, COLS), dt) for dt in (BF16, F32, F32)),
        grid=(2, 2),
        in_specs=[
            pl.BlockSpec(memory_space=pltpu.SMEM),
            pl.BlockSpec(memory_space=pltpu.VMEM),
        ],
        out_specs=(block,) * 3,
        compiler_params=pltpu.CompilerParams(vmem_limit_bytes=VMEM),
        cost_estimate=pl.CostEstimate(flops=12 << 20, bytes_accessed=8 << 20, transcendentals=0),
        name="depth",
    )(depth, received.reshape(2, 2, 32, 80, 128))


def depth_matrix(layer_slot, depth_src, depth_coef):
    hits = (layer_slot[None, None, :] == depth_src[:, :, None]).astype(F32)
    return jnp.sum(depth_coef[:, :, None] * hits, axis=1)


def on_device(small_w, small_m, small_v, width_map, head_map, layer_slot, depth_src, depth_coef):
    z = grow_width(width_map, small_w, small_m, small_v)
    z = z.reshape(32, 2, 128, 128)
    z = lax.all_to_all(z, GROUP, split_axis=0, concat_axis=0, tiled=True)
    y = mix(z, mixing_matrices(head_map))
    received = lax.all_to_all(y, AXES, split_axis=0, concat_axis=0, tiled=True)
    return mix_depth(depth_matrix(layer_slot, depth_src, depth_coef), received)


def solution(mesh):
    chips = Mesh(mesh.devices.reshape(SIZES), AXES)
    grp, fsdp = ("yh", "core"), GROUP
    return jax.shard_map(
        on_device,
        mesh=chips,
        in_specs=(
            P(grp, fsdp, None),
            P(grp, fsdp, None),
            P(grp, fsdp, None),
            P(AXES, None),
            P(),
            P(),
            P(),
            P(),
        ),
        out_specs=(P(None, AXES, None),) * 3,
        check_vma=False,
    )
```

```python
import jax
import jax.numpy as jnp
from jax import lax
from jax.experimental import pallas as pl
from jax.experimental.pallas import tpu as pltpu
from jax.sharding import Mesh, PartitionSpec as P

SIZES = (2, 2, 4, 2, 4)
AXES = ("yh", "core", "x", "yl", "z")
GROUP = ("x", "yl", "z")
BF16, F32 = jnp.bfloat16, jnp.float32

COLS, HALF, DEPTH = 2560, 1280, 4096
BLOCK = 80
UNITS = 64
VMEM = 26 * 1024 * 1024


def place(yh, core, x, yl, z):
    return (((yh * 2 + core) * 4 + x) * 2 + yl) * 4 + z


def shift(value, axis_of_core, by):
    pairs = []
    for yh in range(2):
        for core in range(2):
            for x in range(4):
                for yl in range(2):
                    for z in range(4):
                        to = [x, 2 * yh + yl]
                        to[axis_of_core[core]] = (to[axis_of_core[core]] + by) % 4
                        pairs.append(
                            (place(yh, core, x, yl, z), place(to[1] // 2, core, to[0], to[1] % 2, z))
                        )
    return lax.ppermute(value, AXES, pairs)


def order_kernel(mine, own, before, after, across, out, wide, block, sem):
    for at in range(4):
        for by, shard in ((0, own), (1, after), (2, across), (3, before)):

            @pl.when((at - mine[0] + 4) % 4 == by)
            def _():
                wide[20 * at : 20 * at + 20, :] = shard[...].astype(F32)

    block[...] = wide[...].astype(BF16)
    copy = pltpu.make_async_copy(block, out, sem)
    copy.start()
    copy.wait()


def in_order(mine, *shards):
    whole = pl.BlockSpec(memory_space=pltpu.VMEM)
    return pl.pallas_call(
        order_kernel,
        out_shape=jax.ShapeDtypeStruct((BLOCK, DEPTH), BF16),
        in_specs=[pl.BlockSpec(memory_space=pltpu.SMEM)] + [whole] * 4,
        out_specs=pl.BlockSpec(memory_space=pltpu.HBM),
        scratch_shapes=[
            pltpu.VMEM((BLOCK, DEPTH), F32),
            pltpu.VMEM((BLOCK, DEPTH), BF16),
            pltpu.SemaphoreType.DMA,
        ],
        compiler_params=pltpu.CompilerParams(vmem_limit_bytes=VMEM),
        name="order",
    )(mine, *shards)


def once(value, *done):
    return lax.optimization_barrier((value, *done))[0]


def grow_width(shard, small_w, small_m, small_v):
    core, z = lax.axis_index("core"), lax.axis_index("z")
    x = lax.axis_index("x")
    y = lax.axis_index("yh") * 2 + lax.axis_index("yl")
    q, p = jnp.where(core == 0, x, y), jnp.where(core == 0, y, x)

    def along_p(value, by):
        return shift(value, (1, 0), by)

    def along_q(value, by):
        return shift(value, (0, 1), by)

    def along_z(value, by):
        return lax.ppermute(value, "z", [(i, (i + by) % 4) for i in range(4)])

    before, after, across = along_p(shard, 1), along_p(shard, -1), along_p(shard, 2)
    own = jnp.concatenate([small_w, small_m.astype(BF16), small_v.astype(BF16)], axis=0)
    other = lax.ppermute(own, "core", ((0, 1), (1, 0)))
    a = in_order(p.reshape(1), shard, before, after, across)
    a_before, a_after = along_q(a, 1), along_q(a, -1)
    b_before, b_after = along_z(a, 1), along_z(a, -1)
    a_across = along_q(a_before, 1)
    b = once(jnp.concatenate([b_before, b_after], axis=0), a_before, a_after, other)
    d = along_z(once(a, b_before), 2)
    b_before, b_after = along_q(b, 1), along_q(b, -1)
    here = jnp.stack([core, q, z]).astype(jnp.int32)
    first = (
        (a, b, a_before, a_after, a_across),
        ((0, 0), (0, -1), (0, 1), (-1, 0), (1, 0), (2, 0)),
    )
    z_first = widen(own, other, first)
    d_sent = once(d, z_first)
    d_before, d_after = along_q(d_sent, 1), along_q(d_sent, -1)
    second = ((d, b_before, b_after), ((0, 2), (-1, -1), (-1, 1), (1, -1), (1, 1)))
    b_across = along_q(b_after, -1)
    z_second = widen(own, other, second)
    d_across = along_q(once(d_before, z_second), 1)
    last = (
        (b_across, d_before, d_after, d_across),
        ((2, -1), (2, 1), (-1, 2), (1, 2), (2, 2)),
    )
    partial = spread((first[1], second[1]), (z_first, z_second), here)
    return widen_last(own, other, last, partial, here)


def load_and_project(own, other, pieces, b_ref, a_ref, b_sem, a_sem):
    copies = []
    row = 0
    for i, piece in enumerate(pieces):
        rows = piece.shape[0]
        copies.append(pltpu.make_async_copy(piece, b_ref.at[pl.ds(row, rows)], b_sem.at[i]))
        row += rows
    for i, (src, dst) in enumerate(
        (
            (own.at[0:2], a_ref.at[0:2]),
            (other.at[0:2], a_ref.at[2:4]),
            (own.at[2:3], a_ref.at[4:5]),
            (other.at[2:3], a_ref.at[5:6]),
        )
    ):
        copies.append(pltpu.make_async_copy(src, dst, a_sem.at[i]))
    for copy in copies:
        copy.start()
    for copy in copies:
        copy.wait()
    nt = (((1,), (1,)), ((), ()))
    b = b_ref[...]
    wm = lax.dot_general(a_ref[0:4].reshape(512, DEPTH), b, nt, preferred_element_type=F32)
    v = lax.dot_general(a_ref[4:6].reshape(256, DEPTH), b * b, nt, preferred_element_type=F32)
    return wm.astype(BF16), v.astype(BF16)


def widen_kernel(n, own, other, *refs):
    wm, v = load_and_project(own, other, refs[:n], *refs[n + 1 :])
    refs[n][0:512] = wm
    refs[n][512:768] = v


def spread_columns(places, values, here, previous, out):
    core, q, z = here[0], here[1], here[2]
    row = lax.broadcasted_iota(jnp.int32, (BLOCK, 256), 0)
    lane = lax.broadcasted_iota(jnp.int32, (BLOCK, 256), 1)
    third = [(row >= 20 * k).astype(jnp.int32) for k in (1, 2, 3)]
    line = third[0] + third[1] + third[2]
    inner = row - 20 * line
    spot = (
        inner
        + jnp.where(core == 0, third[1] * 640 + (line - 2 * third[1]) * 80, line * 160)
        - lane
    )

    @pl.loop(0, HALF // 256)
    def _(tile):
        total = None
        for group, value in zip(places, values):
            ones = []
            for dq, dz in group:
                bq, bz = lax.rem(q + dq + 4, 4), lax.rem(z + dz + 4, 4)
                base = bz * 20 + jnp.where(
                    core == 0, bq * 160, (bq // 2) * 640 + lax.rem(bq, 2) * 80
                )
                ones.append(jnp.where(spot == tile * 256 - base, 1.0, 0.0).astype(BF16))
            moved = jnp.dot(
                value[...], jnp.concatenate(ones, axis=0), preferred_element_type=F32
            )
            total = moved if total is None else total + moved
        total = total.astype(BF16)
        for first, at in ((0, 0), (10, 1), (20, 4), (30, 2), (40, 3), (50, 5)):
            for half in range(2):
                t = first + tile * 2 + half
                part = total[at * 128 : at * 128 + 128, half * 128 : half * 128 + 128]
                out[t] = part if previous is None else previous[t] + part

    out[60:64] = jnp.zeros((4, 128, 128), BF16)


def spread(places, values, here):
    def kernel(here, *refs):
        spread_columns(places, refs[:-1], here, None, refs[-1])

    whole = pl.BlockSpec(memory_space=pltpu.VMEM)
    rows = BLOCK * sum(len(group) for group in places)
    return pl.pallas_call(
        kernel,
        out_shape=jax.ShapeDtypeStruct((UNITS, 128, 128), BF16),
        in_specs=[pl.BlockSpec(memory_space=pltpu.SMEM)] + [whole] * len(values),
        out_specs=whole,
        compiler_params=pltpu.CompilerParams(vmem_limit_bytes=VMEM),
        cost_estimate=pl.CostEstimate(
            flops=2 * 768 * rows * HALF, bytes_accessed=4 << 20, transcendentals=0
        ),
        name="spread",
    )(here, *values)


def last_kernel(n, places, here, own, other, *refs):
    last = refs[-1]
    wm, v = load_and_project(own, other, refs[:n], *refs[n + 2 : -1])
    last[0:512] = wm
    last[512:768] = v
    spread_columns([places], [last], here, refs[n], refs[n + 1])


def project_call(kernel, operands, specs, out, rows, n, more_scratch, flops, name):
    return pl.pallas_call(
        kernel,
        out_shape=jax.ShapeDtypeStruct(out, BF16),
        in_specs=specs,
        out_specs=pl.BlockSpec(memory_space=pltpu.VMEM),
        scratch_shapes=[
            pltpu.VMEM((rows, DEPTH), BF16),
            pltpu.VMEM((6, 128, DEPTH), BF16),
            pltpu.SemaphoreType.DMA((n,)),
            pltpu.SemaphoreType.DMA((4,)),
            *more_scratch,
        ],
        compiler_params=pltpu.CompilerParams(vmem_limit_bytes=VMEM),
        cost_estimate=pl.CostEstimate(
            flops=2 * 768 * rows * DEPTH + flops, bytes_accessed=10 << 20, transcendentals=0
        ),
        name=name,
    )(*operands)


def widen(own, other, group):
    pieces, places = group
    n, rows = len(pieces), len(places) * BLOCK

    def kernel(*refs):
        widen_kernel(n, *refs)

    return project_call(
        kernel,
        (own, other, *pieces),
        [pl.BlockSpec(memory_space=pl.ANY)] * (2 + n),
        (768, rows),
        rows,
        n,
        (),
        0,
        "widen",
    )


def widen_last(own, other, group, partial, here):
    pieces, places = group
    n, rows = len(pieces), len(places) * BLOCK

    def kernel(*refs):
        last_kernel(n, places, *refs)

    whole = pl.BlockSpec(memory_space=pltpu.VMEM)
    return project_call(
        kernel,
        (here, own, other, *pieces, partial),
        [pl.BlockSpec(memory_space=pltpu.SMEM)] + [pl.BlockSpec(memory_space=pl.ANY)] * (2 + n) + [whole],
        (UNITS, 128, 128),
        rows,
        n,
        (pltpu.VMEM((768, rows), BF16),),
        2 * 768 * HALF * rows,
        "widen_last",
    )


def mix_kernel(z_ref, m_ref, out, y_ref):
    row = pl.multiple_of(pl.program_id(0) * 32, 32)
    for k in range(2):
        block = jnp.concatenate(
            [z_ref[:, k, pl.ds(row + 16 * i, 16), :].reshape(512, 128) for i in range(2)], axis=1
        )
        y = jnp.dot(m_ref[0], block, preferred_element_type=F32)
        y = y + jnp.dot(m_ref[1], block, preferred_element_type=F32)
        for g in range(40):
            for i in range(2):
                y_ref[k, pl.ds(g * 128 + row + 16 * i, 16), :] = y[
                    g * 16 : g * 16 + 16, i * 128 : i * 128 + 128
                ]

    @pl.when(pl.program_id(0) == 3)
    def _():
        @pl.loop(0, 128, unroll=8)
        def _(d):
            first = pl.multiple_of(d * 40, 8)
            both = jnp.concatenate([y_ref[k, pl.ds(first, 40), :] for k in range(2)], axis=0)
            out[d] = both.astype(BF16)


def mix(z, matrices):
    return pl.pallas_call(
        mix_kernel,
        out_shape=jax.ShapeDtypeStruct((128, 80, 128), BF16),
        grid=(4,),
        in_specs=[
            pl.BlockSpec(memory_space=pltpu.VMEM),
            pl.BlockSpec(memory_space=pltpu.VMEM),
        ],
        out_specs=pl.BlockSpec(memory_space=pltpu.VMEM),
        scratch_shapes=[pltpu.VMEM((2, 5120, 128), F32)],
        compiler_params=pltpu.CompilerParams(vmem_limit_bytes=VMEM),
        cost_estimate=pl.CostEstimate(
            flops=16 * 4 * 640 * 512 * 128, bytes_accessed=8 << 20, transcendentals=0
        ),
        name="mix",
    )(z, matrices)


def matrix_kernel(squared, head, out):
    h = head[...]
    h = jnp.where(squared[0] == 1, h * h, h)
    high = h.astype(BF16)
    low = (h - high.astype(F32)).astype(BF16)

    def iota(shape, dim):
        return lax.broadcasted_iota(jnp.int32, shape, dim)

    down = (iota((640, 40), 0) // 16 == iota((640, 40), 1)).astype(BF16)
    along = (iota((32, 512), 1) // 16 == iota((32, 512), 0)).astype(BF16)
    same = iota((640, 512), 0) % 16 == iota((640, 512), 1) % 16
    for i, part in enumerate((high, low)):
        tall = jnp.dot(down, part, preferred_element_type=F32).astype(BF16)
        full = jnp.dot(tall, along, preferred_element_type=F32)
        out[i] = jnp.where(same, full, 0.0).astype(BF16)


def mixing_matrices(head_map):
    f = (lax.axis_index("x") * 2 + lax.axis_index("yl")) * 4 + lax.axis_index("z")
    squared = ((2 * f % 30) // 10 == 2).astype(jnp.int32).reshape(1)
    whole = pl.BlockSpec(memory_space=pltpu.VMEM)
    return pl.pallas_call(
        matrix_kernel,
        out_shape=jax.ShapeDtypeStruct((2, 640, 512), BF16),
        in_specs=[pl.BlockSpec(memory_space=pltpu.SMEM), whole],
        out_specs=whole,
        compiler_params=pltpu.CompilerParams(vmem_limit_bytes=VMEM),
        name="matrices",
    )(squared, head_map)


def depth_kernel(depth, r_ref, out_w, out_m, out_v):
    core = pl.program_id(0)
    for y_half in range(2):

        @pl.when(pl.program_id(1) == y_half)
        def _():
            for i in range(5):
                pair, k = divmod(y_half * 5 + i, 2)
                for tensor, out in enumerate((out_w, out_m, out_v)):
                    values = [
                        r_ref[yh, core, rel * 15 + tensor * 5 + pair].astype(F32)[k * 40 : k * 40 + 40]
                        for yh in range(2)
                        for rel in range(2)
                    ]
                    for j in range(5):
                        total = None
                        for n, value in enumerate(values):
                            yh, rel = divmod(n, 2)
                            c = depth[j, 2 * yh + lax.rem(rel + core, 2)]
                            c = c * c if tensor == 2 else c
                            total = c * value if total is None else total + c * value
                        out[j, :, i * 128 : i * 128 + 128] = total.astype(out.dtype)


def mix_depth(depth, received):
    block = pl.BlockSpec((5, 40, 640), lambda core, y_half: (0, 0, 2 * y_half + core))
    return pl.pallas_call(
        depth_kernel,
        out_shape=tuple(jax.ShapeDtypeStruct((5, 40, COLS), dt) for dt in (BF16, F32, F32)),
        grid=(2, 2),
        in_specs=[
            pl.BlockSpec(memory_space=pltpu.SMEM),
            pl.BlockSpec(memory_space=pltpu.VMEM),
        ],
        out_specs=(block,) * 3,
        compiler_params=pltpu.CompilerParams(vmem_limit_bytes=VMEM),
        cost_estimate=pl.CostEstimate(flops=12 << 20, bytes_accessed=8 << 20, transcendentals=0),
        name="depth",
    )(depth, received.reshape(2, 2, 32, 80, 128))


def depth_matrix(layer_slot, depth_src, depth_coef):
    hits = (layer_slot[None, None, :] == depth_src[:, :, None]).astype(F32)
    return jnp.sum(depth_coef[:, :, None] * hits, axis=1)


def on_device(small_w, small_m, small_v, width_map, head_map, layer_slot, depth_src, depth_coef):
    z = grow_width(width_map, small_w, small_m, small_v)
    z = z.reshape(32, 2, 128, 128)
    z = lax.all_to_all(z, GROUP, split_axis=0, concat_axis=0, tiled=True)
    y = mix(z, mixing_matrices(head_map))
    received = lax.all_to_all(y, AXES, split_axis=0, concat_axis=0, tiled=True)
    return mix_depth(depth_matrix(layer_slot, depth_src, depth_coef), received)


def solution(mesh):
    chips = Mesh(mesh.devices.reshape(SIZES), AXES)
    grp, fsdp = ("yh", "core"), GROUP
    return jax.shard_map(
        on_device,
        mesh=chips,
        in_specs=(
            P(grp, fsdp, None),
            P(grp, fsdp, None),
            P(grp, fsdp, None),
            P(AXES, None),
            P(),
            P(),
            P(),
            P(),
        ),
        out_specs=(P(None, AXES, None),) * 3,
        check_vma=False,
    )
```

```python
import jax
import jax.numpy as jnp
from jax import lax
from jax.experimental import pallas as pl
from jax.experimental.pallas import tpu as pltpu
from jax.sharding import Mesh, PartitionSpec as P

SIZES = (2, 2, 4, 2, 4)
AXES = ("yh", "core", "x", "yl", "z")
GROUP = ("x", "yl", "z")
BF16, F32 = jnp.bfloat16, jnp.float32

COLS, HALF, DEPTH = 2560, 1280, 4096
BLOCK = 80
UNITS = 64
VMEM = 26 * 1024 * 1024


def place(yh, core, x, yl, z):
    return (((yh * 2 + core) * 4 + x) * 2 + yl) * 4 + z


def shift(value, axis_of_core, by):
    pairs = []
    for yh in range(2):
        for core in range(2):
            for x in range(4):
                for yl in range(2):
                    for z in range(4):
                        to = [x, 2 * yh + yl]
                        to[axis_of_core[core]] = (to[axis_of_core[core]] + by) % 4
                        pairs.append(
                            (place(yh, core, x, yl, z), place(to[1] // 2, core, to[0], to[1] % 2, z))
                        )
    return lax.ppermute(value, AXES, pairs)


def order_kernel(mine, own, before, after, across, out, wide, block, sem):
    for at in range(4):
        for by, shard in ((0, own), (1, after), (2, across), (3, before)):

            @pl.when((at - mine[0] + 4) % 4 == by)
            def _():
                wide[20 * at : 20 * at + 20, :] = shard[...].astype(F32)

    block[...] = wide[...].astype(BF16)
    copy = pltpu.make_async_copy(block, out, sem)
    copy.start()
    copy.wait()


def in_order(mine, *shards):
    whole = pl.BlockSpec(memory_space=pltpu.VMEM)
    return pl.pallas_call(
        order_kernel,
        out_shape=jax.ShapeDtypeStruct((BLOCK, DEPTH), BF16),
        in_specs=[pl.BlockSpec(memory_space=pltpu.SMEM)] + [whole] * 4,
        out_specs=pl.BlockSpec(memory_space=pltpu.HBM),
        scratch_shapes=[
            pltpu.VMEM((BLOCK, DEPTH), F32),
            pltpu.VMEM((BLOCK, DEPTH), BF16),
            pltpu.SemaphoreType.DMA,
        ],
        compiler_params=pltpu.CompilerParams(vmem_limit_bytes=VMEM),
        name="order",
    )(mine, *shards)


def once(value, *done):
    return lax.optimization_barrier((value, *done))[0]


def grow_width(shard, small_w, small_m, small_v):
    core, z = lax.axis_index("core"), lax.axis_index("z")
    x = lax.axis_index("x")
    y = lax.axis_index("yh") * 2 + lax.axis_index("yl")
    q, p = jnp.where(core == 0, x, y), jnp.where(core == 0, y, x)

    def along_p(value, by):
        return shift(value, (1, 0), by)

    def along_q(value, by):
        return shift(value, (0, 1), by)

    def along_z(value, by):
        return lax.ppermute(value, "z", [(i, (i + by) % 4) for i in range(4)])

    before, after, across = along_p(shard, 1), along_p(shard, -1), along_p(shard, 2)
    own = jnp.concatenate([small_w, small_m.astype(BF16), small_v.astype(BF16)], axis=0)
    other = lax.ppermute(own, "core", ((0, 1), (1, 0)))
    a = in_order(p.reshape(1), shard, before, after, across)
    a_before, a_after = along_q(a, 1), along_q(a, -1)
    b_before, b_after = along_z(a, 1), along_z(a, -1)
    a_across = along_q(a_before, 1)
    b = once(jnp.concatenate([b_before, b_after], axis=0), a_before, a_after, other)
    d = along_z(once(a, b_before), 2)
    b_before, b_after = along_q(b, 1), along_q(b, -1)
    here = jnp.stack([core, q, z]).astype(jnp.int32)
    first = (
        (a, b, a_before, a_after, a_across),
        ((0, 0), (0, -1), (0, 1), (-1, 0), (1, 0), (2, 0)),
    )
    z_first = widen(own, other, first)
    d_sent = once(d, z_first)
    d_before, d_after = along_q(d_sent, 1), along_q(d_sent, -1)
    second = ((d, b_before, b_after), ((0, 2), (-1, -1), (-1, 1), (1, -1), (1, 1)))
    b_across = along_q(b_after, -1)
    z_second = widen(own, other, second)
    d_across = along_q(once(d_before, z_second), 1)
    last = (
        (b_across, d_before, d_after, d_across),
        ((2, -1), (2, 1), (-1, 2), (1, 2), (2, 2)),
    )
    partial = spread((first[1], second[1]), (z_first, z_second), here)
    return widen_last(own, other, last, partial, here)


def load_and_project(own, other, pieces, b_ref, a_ref, b_sem, a_sem):
    copies = []
    row = 0
    for i, piece in enumerate(pieces):
        rows = piece.shape[0]
        copies.append(pltpu.make_async_copy(piece, b_ref.at[pl.ds(row, rows)], b_sem.at[i]))
        row += rows
    for i, (src, dst) in enumerate(
        (
            (own.at[0:2], a_ref.at[0:2]),
            (other.at[0:2], a_ref.at[2:4]),
            (own.at[2:3], a_ref.at[4:5]),
            (other.at[2:3], a_ref.at[5:6]),
        )
    ):
        copies.append(pltpu.make_async_copy(src, dst, a_sem.at[i]))
    for copy in copies:
        copy.start()
    for copy in copies:
        copy.wait()
    nt = (((1,), (1,)), ((), ()))
    b = b_ref[...]
    wm = lax.dot_general(a_ref[0:4].reshape(512, DEPTH), b, nt, preferred_element_type=F32)
    v = lax.dot_general(a_ref[4:6].reshape(256, DEPTH), b * b, nt, preferred_element_type=F32)
    return wm.astype(BF16), v.astype(BF16)


def widen_kernel(n, own, other, *refs):
    wm, v = load_and_project(own, other, refs[:n], *refs[n + 1 :])
    refs[n][0:512] = wm
    refs[n][512:768] = v


def spread_columns(places, values, here, previous, out):
    core, q, z = here[0], here[1], here[2]
    row = lax.broadcasted_iota(jnp.int32, (BLOCK, 256), 0)
    lane = lax.broadcasted_iota(jnp.int32, (BLOCK, 256), 1)
    third = [(row >= 20 * k).astype(jnp.int32) for k in (1, 2, 3)]
    line = third[0] + third[1] + third[2]
    inner = row - 20 * line
    spot = (
        inner
        + jnp.where(core == 0, third[1] * 640 + (line - 2 * third[1]) * 80, line * 160)
        - lane
    )

    @pl.loop(0, HALF // 256)
    def _(tile):
        total = None
        for group, value in zip(places, values):
            ones = []
            for dq, dz in group:
                bq, bz = lax.rem(q + dq + 4, 4), lax.rem(z + dz + 4, 4)
                base = bz * 20 + jnp.where(
                    core == 0, bq * 160, (bq // 2) * 640 + lax.rem(bq, 2) * 80
                )
                ones.append(jnp.where(spot == tile * 256 - base, 1.0, 0.0).astype(BF16))
            moved = jnp.dot(
                value[...], jnp.concatenate(ones, axis=0), preferred_element_type=F32
            )
            total = moved if total is None else total + moved
        total = total.astype(BF16)
        for first, at in ((0, 0), (10, 1), (20, 4), (30, 2), (40, 3), (50, 5)):
            for half in range(2):
                t = first + tile * 2 + half
                part = total[at * 128 : at * 128 + 128, half * 128 : half * 128 + 128]
                out[t] = part if previous is None else previous[t] + part

    out[60:64] = jnp.zeros((4, 128, 128), BF16)


def spread(places, values, here):
    def kernel(here, *refs):
        spread_columns(places, refs[:-1], here, None, refs[-1])

    whole = pl.BlockSpec(memory_space=pltpu.VMEM)
    rows = BLOCK * sum(len(group) for group in places)
    return pl.pallas_call(
        kernel,
        out_shape=jax.ShapeDtypeStruct((UNITS, 128, 128), BF16),
        in_specs=[pl.BlockSpec(memory_space=pltpu.SMEM)] + [whole] * len(values),
        out_specs=whole,
        compiler_params=pltpu.CompilerParams(vmem_limit_bytes=VMEM),
        cost_estimate=pl.CostEstimate(
            flops=2 * 768 * rows * HALF, bytes_accessed=4 << 20, transcendentals=0
        ),
        name="spread",
    )(here, *values)


def last_kernel(n, places, here, own, other, *refs):
    last = refs[-1]
    wm, v = load_and_project(own, other, refs[:n], *refs[n + 2 : -1])
    last[0:512] = wm
    last[512:768] = v
    spread_columns([places], [last], here, refs[n], refs[n + 1])


def project_call(kernel, operands, specs, out, rows, n, more_scratch, flops, name):
    return pl.pallas_call(
        kernel,
        out_shape=jax.ShapeDtypeStruct(out, BF16),
        in_specs=specs,
        out_specs=pl.BlockSpec(memory_space=pltpu.VMEM),
        scratch_shapes=[
            pltpu.VMEM((rows, DEPTH), BF16),
            pltpu.VMEM((6, 128, DEPTH), BF16),
            pltpu.SemaphoreType.DMA((n,)),
            pltpu.SemaphoreType.DMA((4,)),
            *more_scratch,
        ],
        compiler_params=pltpu.CompilerParams(vmem_limit_bytes=VMEM),
        cost_estimate=pl.CostEstimate(
            flops=2 * 768 * rows * DEPTH + flops, bytes_accessed=10 << 20, transcendentals=0
        ),
        name=name,
    )(*operands)


def widen(own, other, group):
    pieces, places = group
    n, rows = len(pieces), len(places) * BLOCK

    def kernel(*refs):
        widen_kernel(n, *refs)

    return project_call(
        kernel,
        (own, other, *pieces),
        [pl.BlockSpec(memory_space=pl.ANY)] * (2 + n),
        (768, rows),
        rows,
        n,
        (),
        0,
        "widen",
    )


def widen_last(own, other, group, partial, here):
    pieces, places = group
    n, rows = len(pieces), len(places) * BLOCK

    def kernel(*refs):
        last_kernel(n, places, *refs)

    whole = pl.BlockSpec(memory_space=pltpu.VMEM)
    return project_call(
        kernel,
        (here, own, other, *pieces, partial),
        [pl.BlockSpec(memory_space=pltpu.SMEM)] + [pl.BlockSpec(memory_space=pl.ANY)] * (2 + n) + [whole],
        (UNITS, 128, 128),
        rows,
        n,
        (pltpu.VMEM((768, rows), BF16),),
        2 * 768 * HALF * rows,
        "widen_last",
    )


def mix_kernel(z_ref, m_ref, out, y_ref):
    row = pl.multiple_of(pl.program_id(0) * 32, 32)
    for k in range(2):
        block = jnp.concatenate(
            [z_ref[:, k, pl.ds(row + 16 * i, 16), :].reshape(512, 128) for i in range(2)], axis=1
        )
        y = jnp.dot(m_ref[0], block, preferred_element_type=F32)
        for g in range(40):
            for i in range(2):
                y_ref[k, pl.ds(g * 128 + row + 16 * i, 16), :] = y[
                    g * 16 : g * 16 + 16, i * 128 : i * 128 + 128
                ]

    @pl.when(pl.program_id(0) == 3)
    def _():
        @pl.loop(0, 128, unroll=8)
        def _(d):
            first = pl.multiple_of(d * 40, 8)
            both = jnp.concatenate([y_ref[k, pl.ds(first, 40), :] for k in range(2)], axis=0)
            out[d] = both.astype(BF16)


def mix(z, matrices):
    return pl.pallas_call(
        mix_kernel,
        out_shape=jax.ShapeDtypeStruct((128, 80, 128), BF16),
        grid=(4,),
        in_specs=[
            pl.BlockSpec(memory_space=pltpu.VMEM),
            pl.BlockSpec(memory_space=pltpu.VMEM),
        ],
        out_specs=pl.BlockSpec(memory_space=pltpu.VMEM),
        scratch_shapes=[pltpu.VMEM((2, 5120, 128), F32)],
        compiler_params=pltpu.CompilerParams(vmem_limit_bytes=VMEM),
        cost_estimate=pl.CostEstimate(
            flops=16 * 2 * 640 * 512 * 128, bytes_accessed=8 << 20, transcendentals=0
        ),
        name="mix",
    )(z, matrices)


def matrix_kernel(squared, head, out):
    h = head[...]
    h = jnp.where(squared[0] == 1, h * h, h)

    def iota(shape, dim):
        return lax.broadcasted_iota(jnp.int32, shape, dim)

    down = (iota((640, 40), 0) // 16 == iota((640, 40), 1)).astype(BF16)
    along = (iota((32, 512), 1) // 16 == iota((32, 512), 0)).astype(BF16)
    same = iota((640, 512), 0) % 16 == iota((640, 512), 1) % 16
    tall = jnp.dot(down, h.astype(BF16), preferred_element_type=F32).astype(BF16)
    full = jnp.dot(tall, along, preferred_element_type=F32)
    out[0] = jnp.where(same, full, 0.0).astype(BF16)


def mixing_matrices(head_map):
    f = (lax.axis_index("x") * 2 + lax.axis_index("yl")) * 4 + lax.axis_index("z")
    squared = ((2 * f % 30) // 10 == 2).astype(jnp.int32).reshape(1)
    whole = pl.BlockSpec(memory_space=pltpu.VMEM)
    return pl.pallas_call(
        matrix_kernel,
        out_shape=jax.ShapeDtypeStruct((1, 640, 512), BF16),
        in_specs=[pl.BlockSpec(memory_space=pltpu.SMEM), whole],
        out_specs=whole,
        compiler_params=pltpu.CompilerParams(vmem_limit_bytes=VMEM),
        name="matrices",
    )(squared, head_map)


def depth_kernel(depth, r_ref, out_w, out_m, out_v):
    core = pl.program_id(0)
    for y_half in range(2):

        @pl.when(pl.program_id(1) == y_half)
        def _():
            for i in range(5):
                pair, k = divmod(y_half * 5 + i, 2)
                for tensor, out in enumerate((out_w, out_m, out_v)):
                    values = [
                        r_ref[yh, core, rel * 15 + tensor * 5 + pair].astype(F32)[k * 40 : k * 40 + 40]
                        for yh in range(2)
                        for rel in range(2)
                    ]
                    for j in range(5):
                        total = None
                        for n, value in enumerate(values):
                            yh, rel = divmod(n, 2)
                            c = depth[j, 2 * yh + lax.rem(rel + core, 2)]
                            c = c * c if tensor == 2 else c
                            total = c * value if total is None else total + c * value
                        out[j, :, i * 128 : i * 128 + 128] = total.astype(out.dtype)


def mix_depth(depth, received):
    block = pl.BlockSpec((5, 40, 640), lambda core, y_half: (0, 0, 2 * y_half + core))
    return pl.pallas_call(
        depth_kernel,
        out_shape=tuple(jax.ShapeDtypeStruct((5, 40, COLS), dt) for dt in (BF16, F32, F32)),
        grid=(2, 2),
        in_specs=[
            pl.BlockSpec(memory_space=pltpu.SMEM),
            pl.BlockSpec(memory_space=pltpu.VMEM),
        ],
        out_specs=(block,) * 3,
        compiler_params=pltpu.CompilerParams(vmem_limit_bytes=VMEM),
        cost_estimate=pl.CostEstimate(flops=12 << 20, bytes_accessed=8 << 20, transcendentals=0),
        name="depth",
    )(depth, received.reshape(2, 2, 32, 80, 128))


def depth_matrix(layer_slot, depth_src, depth_coef):
    hits = (layer_slot[None, None, :] == depth_src[:, :, None]).astype(F32)
    return jnp.sum(depth_coef[:, :, None] * hits, axis=1)


def on_device(small_w, small_m, small_v, width_map, head_map, layer_slot, depth_src, depth_coef):
    z = grow_width(width_map, small_w, small_m, small_v)
    z = z.reshape(32, 2, 128, 128)
    z = lax.all_to_all(z, GROUP, split_axis=0, concat_axis=0, tiled=True)
    y = mix(z, mixing_matrices(head_map))
    received = lax.all_to_all(y, AXES, split_axis=0, concat_axis=0, tiled=True)
    return mix_depth(depth_matrix(layer_slot, depth_src, depth_coef), received)


def solution(mesh):
    chips = Mesh(mesh.devices.reshape(SIZES), AXES)
    grp, fsdp = ("yh", "core"), GROUP
    return jax.shard_map(
        on_device,
        mesh=chips,
        in_specs=(
            P(grp, fsdp, None),
            P(grp, fsdp, None),
            P(grp, fsdp, None),
            P(AXES, None),
            P(),
            P(),
            P(),
            P(),
        ),
        out_specs=(P(None, AXES, None),) * 3,
        check_vma=False,
    )
```
